512 devices in a mesh: tm: 32 (over y, x_hi, core), head: 16 (over x_lo, z).
Axes of the slice: x: 4 (x_hi: 2, x_lo: 2; x = x_hi * 2 + x_lo), y: 8, z: 8, core: 2. Of those that a mesh axis runs over, the one named last changes fastest.
Arguments:
- queries: bfloat16 [16384, 3072], P(('tm', 'head')), may hold values from -24 to 24
- key_vectors: bfloat16 [16384, 3072], P(('tm', 'head')), may hold values from -24 to 24
- value_vectors: bfloat16 [16384, 3072], P(('tm', 'head')), may hold values from -6 to 6
- frame_order: int32 [64], replicated, may hold values from 0 to 63, each once
- kept_blocks: int32 [64, 12], replicated, may hold values from -1 to 63, as said below
Outputs:
- attended: bfloat16 [16384, 3072], P(('tm', 'head'))
The draws below stay inside these ranges and needn't reach their ends.
Inputs may be any that keep to these rules, and one draw needn't show every extreme that they name: `kept_blocks`: each row lists distinct frame blocks first and -1 after them; every row lists 4 to 12 blocks, always its own frame block and the frame blocks next to it, and some row lists exactly 12.
All inputs are finite; a program needn't handle non-finite values.
Results may differ from the reference program's by a relative error of at most 0.0085.
Values may be sent and summed in bfloat16 or wider, within the bound.
No kernel may reach another device: no remote copies, remote signals or barrier semaphores. Data moves between devices by JAX's collectives and lax.ppermute only.
A program may use at most 128 MiB of HBM per device.

```python
import jax
import jax.numpy as jnp
from jax import lax

HD = 64
D = 3072
BLOCK = 256
KMAX = 12
NB = 64
TOKENS = 16384


def draw_queries(key, part):
    key = jax.random.fold_in(key, 11)
    return jnp.clip(jax.random.normal(key, (TOKENS, D), jnp.float32), -4.0, 4.0).astype(jnp.bfloat16)


def draw_key_vectors(key, part):
    key = jax.random.fold_in(key, 12)
    return jnp.clip(jax.random.normal(key, (TOKENS, D), jnp.float32), -4.0, 4.0).astype(jnp.bfloat16)


def draw_kept_blocks(key, part):
    key = jax.random.fold_in(key, 5)
    key_one, key_two, key_three = jax.random.split(key, 3)
    query_ids = jnp.arange(NB, dtype=jnp.int32)[:, None]
    column_ids = jnp.arange(NB, dtype=jnp.int32)[None, :]
    distance = jnp.abs(query_ids - column_ids)
    rough = jax.random.randint(key_one, (NB, NB), 1, 65536, dtype=jnp.int32)
    priority = jnp.where(distance <= 1, 1 << 20, rough // (1 + distance))
    ranked = priority * NB + (NB - 1 - column_ids)
    ignored, chosen = lax.top_k(ranked, KMAX)
    listed = jax.random.randint(key_two, (NB,), 4, KMAX + 1, dtype=jnp.int32)
    full_row = jax.random.randint(key_three, (), 0, NB, dtype=jnp.int32)
    listed = jnp.where(jnp.arange(NB, dtype=jnp.int32) == full_row, KMAX, listed)
    slot_ids = jnp.arange(KMAX, dtype=jnp.int32)[None, :]
    return jnp.where(slot_ids < listed[:, None], chosen, -1).astype(jnp.int32)


def block_levels(stream_key, extent, pieces, least, largest):
    gain, own = 1.0, jax.random.fold_in(stream_key, 6)
    for axis_at, shards_of in pieces:
        heights = jnp.exp(jax.random.uniform(jax.random.fold_in(own, axis_at), (shards_of,), jnp.float32, least / len(pieces), largest / len(pieces)))
        gain = gain * jnp.repeat(heights, extent[axis_at] // shards_of).reshape([-1 if axis == axis_at else 1 for axis in range(len(extent))])
    return gain


def gaussian(stream_key, extent, scale, most, pieces=(), kind=jnp.bfloat16):
    values = scale * jax.random.normal(stream_key, extent, jnp.float32)
    if pieces:
        values = values * block_levels(stream_key, extent, pieces, -0.22, 0.18)
    return jnp.clip(values, -most, most).astype(kind)


def setup_inputs(seed: int = 0) -> dict:
    arg_keys = jax.random.split(jax.random.key(seed), 6)
    return {
        "queries": draw_queries(jax.random.fold_in(arg_keys[5], 71), 0),
        "key_vectors": draw_key_vectors(jax.random.fold_in(arg_keys[5], 71), 0),
        "value_vectors": gaussian(arg_keys[2], (TOKENS, D), 1.0, 6.0, ((0, 512),)),
        "frame_order": jax.random.permutation(arg_keys[3], NB).astype(jnp.int32),
        "kept_blocks": draw_kept_blocks(jax.random.fold_in(arg_keys[5], 71), 0),
    }


masked_score = -1.0e30


def kept_positions(frame_order, kept_rows):
    block_ids = jnp.arange(frame_order.shape[0], dtype=jnp.int32)
    matches = frame_order[None, None, :] == kept_rows[:, :, None]
    positions = jnp.sum(jnp.where(matches, block_ids[None, None, :], 0), axis=2).astype(jnp.int32)
    return positions, kept_rows >= 0


def attend_block(query_block, key_set, value_set, usable, score_scale):
    scores = jnp.einsum("qhd,jkhd->qhjk", query_block.astype(jnp.float32), key_set.astype(jnp.float32)) * score_scale
    live = usable[None, None, :, None]
    scores = jnp.where(live, scores, masked_score)
    best = jnp.max(scores, axis=(2, 3), keepdims=True)
    weights = jnp.where(live, jnp.exp(scores - best), 0.0)
    total = jnp.sum(weights, axis=(2, 3))
    rounded = weights.astype(jnp.bfloat16)
    mixed = jnp.einsum("qhjk,jkhd->qhd", rounded.astype(jnp.float32), value_set.astype(jnp.float32))
    return (mixed / total[:, :, None]).astype(jnp.bfloat16)


def reference(queries, key_vectors, value_vectors, frame_order, kept_blocks):
    head_count = D // HD
    block_shape = (NB, BLOCK, head_count, HD)
    query_blocks = queries.reshape(block_shape)
    key_blocks = key_vectors.reshape(block_shape)
    value_blocks = value_vectors.reshape(block_shape)
    positions, usable = kept_positions(frame_order, kept_blocks)

    def one_block(position):
        frame = frame_order[position]
        chosen = positions[frame]
        return attend_block(query_blocks[position], key_blocks[chosen], value_blocks[chosen], usable[frame], HD ** -0.5)

    mixed = lax.map(one_block, jnp.arange(NB, dtype=jnp.int32))
    return mixed.reshape(TOKENS, D)
```

```python
import jax
import jax.numpy as jnp
from jax import lax
from jax.experimental import pallas as pl
from jax.experimental.pallas import tpu as pltpu
from jax.sharding import PartitionSpec as P

HD = 64
BLOCK = 256
HEADS = 48
NB = 64
KMAX = 12
PAIR = 2 * HD
COLS = 64
SLICE = 32
NY = 8
AXES = ("tm", "head")
MASKED = -1e30
UNROLL = 4
STAGE_SHIFT = 6
STAGE_BASE = 1 << STAGE_SHIFT
LIST = NY * KMAX + UNROLL
EXP2_SCALE = 0.125 * 1.4426950408889634


def flat_index(x, y, z, core):
    return ((y * 2 + (x >> 1)) * 2 + core) * 16 + (x & 1) * 8 + z


COLUMN_GROUPS = [
    [flat_index(x, y, z, c) for y in range(8) for z in range(8)] for x in range(4) for c in range(2)
]


def moves(target):
    return [
        (flat_index(x, y, z, c), flat_index(target(x, c)[0], y, z, target(x, c)[1]))
        for x in range(4)
        for y in range(8)
        for z in range(8)
        for c in range(2)
    ]


SWAP_CORES = moves(lambda x, c: (x, 1 - c))
ONWARD = moves(lambda x, c: ((x + 1 - 2 * c) % 4, c))


def low_lanes(shape):
    return lax.broadcasted_iota(jnp.int32, shape, len(shape) - 1) < HD


def pack_kernel(q_ref, k_ref, v_ref, out_ref):
    low = low_lanes((SLICE, PAIR))
    low_half = low_lanes((SLICE // 2, PAIR))
    half = SLICE // 2
    for pair in range(HEADS // 2):
        lanes = pl.ds(pair * PAIR, PAIR)
        k, v, q = k_ref[:, lanes], v_ref[:, lanes], q_ref[:, lanes]
        k_swap, v_swap, q_swap = (jnp.concatenate([t[:, HD:], t[:, :HD]], axis=1) for t in (k, v, q))
        even, odd = 2 * pair, 2 * pair + 1
        out_ref[even, :SLICE, :] = jnp.where(low, k, v_swap)
        out_ref[odd, :SLICE, :] = jnp.where(low, k_swap, v)
        out_ref[even, SLICE:, :] = jnp.where(low_half, q[:half], q_swap[half:])
        out_ref[odd, SLICE:, :] = jnp.where(low_half, q_swap[:half], q[half:])
    out_ref[HEADS:] = jnp.zeros((COLS - HEADS, SLICE + half, PAIR), jnp.bfloat16)


def unpack_kernel(in_ref, out_ref):
    half = SLICE // 2
    low = low_lanes((half, PAIR))
    for pair in range(HEADS // 2):
        lanes = pl.ds(pair * PAIR, PAIR)
        even, odd = in_ref[2 * pair], in_ref[2 * pair + 1]
        even_swap, odd_swap = (jnp.concatenate([t[:, HD:], t[:, :HD]], axis=1) for t in (even, odd))
        out_ref[:half, lanes] = jnp.where(low, even, odd_swap)
        out_ref[half:, lanes] = jnp.where(low, even_swap, odd)


def list_pairs(order_ref, kept_ref, place_ref, where_is, pairs_ref, counts_ref):
    x_here, core_here, live = place_ref[0], place_ref[1], place_ref[2]

    def place(p, carry):
        away = (((p >> 2) & 1) * 2 + (p & 1) - x_here) & 3
        core = (p >> 1) & 1
        way = (away >> 1) ^ 1
        near = (way ^ core_here) * 2 + (core ^ way)
        part = jnp.where((away & 1) == 1, STAGE_BASE + near * NY, away * STAGE_BASE + (core ^ core_here) * NY)
        where_is[order_ref[p]] = part + (p >> 3)
        return carry

    lax.fori_loop(0, NB, place, 0, unroll=8)

    def list_block(block, ends):
        p = block * NY + (x_here >> 1) * 4 + core_here * 2 + (x_here & 1)
        frame = order_ref[p]
        for j in range(KMAX):
            kept = kept_ref[j, frame]
            there = where_is[jnp.maximum(kept, 0)]
            stage = there >> STAGE_SHIFT
            end = jnp.where(stage == 0, ends[0], jnp.where(stage == 1, ends[1], ends[2]))
            pairs_ref[end] = block * STAGE_BASE + (there & (STAGE_BASE - 1))
            ends = tuple(
                e + ((kept >= 0) & (stage == k)).astype(jnp.int32) for k, e in enumerate(ends)
            )
        return ends

    starts = tuple(stage * LIST for stage in range(3))
    ends = lax.fori_loop(0, NY * live, list_block, tuple(jnp.int32(k) for k in starts))
    for stage in range(3):
        counts_ref[stage] = ends[stage] - starts[stage]
        for u in range(UNROLL):
            pairs_ref[ends[stage] + u] = NY * STAGE_BASE


def spread_queries(mine_ref, q_ref):
    half = SLICE // 2
    for block in range(NY):
        packed = mine_ref[pl.ds(block * NY, NY), SLICE:, :]
        low = low_lanes(packed.shape)
        swapped = jnp.concatenate([packed[:, :, HD:], packed[:, :, :HD]], axis=2)
        zero = jnp.zeros_like(packed)
        q = jnp.concatenate([jnp.where(low, packed, zero), jnp.where(low, swapped, zero)], axis=1)
        q_ref[block] = q.reshape(NY * 2 * half, PAIR)


def add_pairs(stage, pairs_ref, counts_ref, q_ref, kv, best_in, best, mixed_in, mixed, scores, top):
    steps = (counts_ref[stage] + UNROLL - 1) // UNROLL

    def pair(t, u):
        j = t * UNROLL + u
        both = pairs_ref[stage * LIST + j]
        return j, both >> STAGE_SHIFT, both & (STAGE_BASE - 1)

    if best_in is None:
        for block in range(NY + 1):
            top[block] = jnp.full((BLOCK, PAIR), MASKED, jnp.float32)
            mixed[block] = jnp.zeros((BLOCK, PAIR), jnp.float32)
    else:
        for block in range(NY):
            top[block] = best_in[block]

    @pl.loop(0, steps)
    def _(t):
        for u in range(UNROLL):
            j, block, row = pair(t, u)
            s = lax.dot_general(
                q_ref[block], kv[row], (((1,), (1,)), ((), ())), preferred_element_type=jnp.float32
            )
            scores[j] = s
            top[block] = jnp.maximum(top[block], jnp.maximum(s[:, :PAIR], s[:, PAIR:]))

    for block in range(NY):
        new = jnp.broadcast_to(jnp.max(top[block], axis=1, keepdims=True), (BLOCK, PAIR))
        if best_in is not None:
            mixed[block] = mixed_in[block] * jnp.exp2((best_in[block] - new) * EXP2_SCALE)
        best[block] = new

    low = low_lanes((BLOCK, PAIR))

    @pl.loop(0, steps)
    def _(t):
        for u in range(UNROLL):
            j, block, row = pair(t, u)
            peak = best[block]
            s = scores[j]
            weights = jnp.concatenate([s[:, :PAIR] - peak, s[:, PAIR:] - peak], axis=1)
            weights = jnp.exp2(weights * EXP2_SCALE).astype(jnp.bfloat16)
            values = jnp.where(low, jnp.ones((), jnp.bfloat16), kv[row])
            mixed[block] += jnp.dot(weights, values, preferred_element_type=jnp.float32)


def fetch(kv_refs, kv, sems):
    copies = [
        pltpu.make_async_copy(ref, kv.at[pl.ds(i * NY, NY)], sems.at[i]) for i, ref in enumerate(kv_refs)
    ]
    for copy in copies:
        copy.start()
    return copies


def first_kernel(order_ref, kept_ref, place_ref, mine_ref, own_ref, twin_ref, *refs):
    best, mixed, q_ref, pairs_ref, counts_ref, kv, scores, top, where_is, sems = refs
    copies = fetch((own_ref, twin_ref), kv, sems)
    list_pairs(order_ref, kept_ref, place_ref, where_is, pairs_ref, counts_ref)
    spread_queries(mine_ref, q_ref)
    q_ref[NY] = jnp.zeros((BLOCK, PAIR), jnp.bfloat16)
    best[NY] = jnp.zeros((BLOCK, PAIR), jnp.float32)
    for copy in copies:
        copy.wait()
    add_pairs(0, pairs_ref, counts_ref, q_ref, kv, None, best, None, mixed, scores, top)


def second_kernel(pairs_ref, counts_ref, q_ref, best_in, mixed_in, *refs):
    kv_refs = refs[:4]
    best, mixed, kv, scores, top, sems = refs[4:]
    for copy in fetch(kv_refs, kv, sems):
        copy.wait()
    mixed[NY] = jnp.zeros((BLOCK, PAIR), jnp.float32)
    best[NY] = jnp.zeros((BLOCK, PAIR), jnp.float32)
    top[NY] = jnp.zeros((BLOCK, PAIR), jnp.float32)
    add_pairs(1, pairs_ref, counts_ref, q_ref, kv, best_in, best, mixed_in, mixed, scores, top)


def last_kernel(pairs_ref, counts_ref, q_ref, best_in, mixed_in, *refs):
    kv_refs = refs[:2]
    out_ref, best, mixed, kv, scores, top, sems = refs[2:]
    for copy in fetch(kv_refs, kv, sems):
        copy.wait()
    mixed[NY] = jnp.zeros((BLOCK, PAIR), jnp.float32)
    best[NY] = jnp.zeros((BLOCK, PAIR), jnp.float32)
    top[NY] = jnp.zeros((BLOCK, PAIR), jnp.float32)
    add_pairs(2, pairs_ref, counts_ref, q_ref, kv, best_in, best, mixed_in, mixed, scores, top)
    half = SLICE // 2
    low = low_lanes((NY, half, PAIR))
    for block in range(NY):
        both = mixed[block]
        done = both / jnp.concatenate([both[:, HD:], both[:, :HD]], axis=1)
        done = done.reshape(NY, SLICE, PAIR)
        first, second = done[:, :half], done[:, half:]
        first = jnp.concatenate([first[:, :, HD:], first[:, :, :HD]], axis=2)
        out_ref[pl.ds(block * NY, NY)] = jnp.where(low, first, second).astype(jnp.bfloat16)


VMEM = pl.BlockSpec(memory_space=pltpu.VMEM)
SMEM = pl.BlockSpec(memory_space=pltpu.SMEM)
ANY = pl.BlockSpec(memory_space=pl.ANY)


def pack(q, k, v):
    return pl.pallas_call(
        pack_kernel,
        out_shape=jax.ShapeDtypeStruct((COLS, SLICE + SLICE // 2, PAIR), jnp.bfloat16),
        in_specs=[VMEM] * 3,
        out_specs=VMEM,
        name="pack",
    )(q, k, v)


def unpack(mixed):
    return pl.pallas_call(
        unpack_kernel,
        out_shape=jax.ShapeDtypeStruct((SLICE, HEADS * HD), jnp.bfloat16),
        in_specs=[VMEM],
        out_specs=VMEM,
        name="unpack",
    )(mixed)


STATE = jax.ShapeDtypeStruct((NY + 1, BLOCK, PAIR), jnp.float32)


def stage_scratch(chunks):
    return [
        pltpu.VMEM((chunks * NY, BLOCK, PAIR), jnp.bfloat16),
        pltpu.VMEM((NY * KMAX + UNROLL, BLOCK, BLOCK), jnp.float32),
        pltpu.VMEM((NY + 1, BLOCK, PAIR), jnp.float32),
    ]


def stage_options(share):
    return dict(
        compiler_params=pltpu.CompilerParams(vmem_limit_bytes=44 * 1024 * 1024),
        cost_estimate=pl.CostEstimate(flops=share, bytes_accessed=share, transcendentals=share),
    )


def attend_first(order, kept, place, mine, own, twin):
    return pl.pallas_call(
        first_kernel,
        out_shape=(
            STATE,
            STATE,
            jax.ShapeDtypeStruct((NY + 1, BLOCK, PAIR), jnp.bfloat16),
            jax.ShapeDtypeStruct((3 * LIST,), jnp.int32),
            jax.ShapeDtypeStruct((3,), jnp.int32),
        ),
        in_specs=[SMEM] * 3 + [VMEM] + [ANY] * 2,
        out_specs=(VMEM, VMEM, VMEM, SMEM, SMEM),
        scratch_shapes=stage_scratch(2) + [pltpu.SMEM((NB,), jnp.int32), pltpu.SemaphoreType.DMA((2,))],
        name="attend_own",
        **stage_options(1),
    )(order, kept, place, mine, own, twin)


def attend_second(pairs, counts, q, best, mixed, near):
    return pl.pallas_call(
        second_kernel,
        out_shape=(STATE, STATE),
        in_specs=[SMEM] * 2 + [VMEM] * 3 + [ANY] * 4,
        out_specs=(VMEM, VMEM),
        scratch_shapes=stage_scratch(4) + [pltpu.SemaphoreType.DMA((4,))],
        input_output_aliases={3: 0, 4: 1},
        name="attend_near",
        **stage_options(2),
    )(pairs, counts, q, best, mixed, *near)


def attend_last(pairs, counts, q, best, mixed, far):
    return pl.pallas_call(
        last_kernel,
        out_shape=jax.ShapeDtypeStruct((COLS, SLICE // 2, PAIR), jnp.bfloat16),
        in_specs=[SMEM] * 2 + [VMEM] * 3 + [ANY] * 2,
        out_specs=VMEM,
        scratch_shapes=[pltpu.VMEM((NY + 1, BLOCK, PAIR), jnp.float32)] * 2
        + stage_scratch(2)
        + [pltpu.SemaphoreType.DMA((2,))],
        name="attend_far",
        **stage_options(1),
    )(pairs, counts, q, best, mixed, *far)


def local(queries, key_vectors, value_vectors, frame_order, kept_blocks):
    tm, head = lax.axis_index("tm"), lax.axis_index("head")
    x_here = ((tm >> 1) & 1) * 2 + (head >> 3)
    column = (tm >> 2) * 8 + (head & 7)
    place = jnp.stack([x_here, tm & 1, (column < HEADS).astype(jnp.int32)]).astype(jnp.int32)
    packed = pack(queries, key_vectors, value_vectors)
    mine = lax.all_to_all(packed, AXES, 0, 0, tiled=True, axis_index_groups=COLUMN_GROUPS)
    kv = mine[:, :SLICE].reshape(NY, BLOCK, PAIR)
    swap = lambda t: lax.ppermute(t, AXES, SWAP_CORES)
    onward = lambda t: lax.ppermute(t, AXES, ONWARD)
    near_own = onward(kv)
    twin = swap(kv)
    near_twin = onward(twin)
    far = onward(near_own)
    own, twin, near_own = lax.optimization_barrier((kv, twin, near_own))
    best, mixed, q, pairs, counts = attend_first(frame_order, kept_blocks.T, place, mine, own, twin)
    near_own, near_twin, best, mixed = lax.optimization_barrier((near_own, near_twin, best, mixed))
    near = [near_own, near_twin, swap(near_own), swap(near_twin)]
    best, mixed = attend_second(pairs, counts, q, best, mixed, near)
    mixed = attend_last(pairs, counts, q, best, mixed, [far, swap(far)])
    back = lax.all_to_all(mixed, AXES, 0, 0, tiled=True, axis_index_groups=COLUMN_GROUPS)
    return unpack(back)


def solution(mesh):
    tokens = P(AXES, None)
    return jax.shard_map(
        local, mesh=mesh, in_specs=(tokens, tokens, tokens, P(), P()), out_specs=tokens, check_vma=False
    )
```

```python
import jax
import jax.numpy as jnp
from jax import lax
from jax.experimental import pallas as pl
from jax.experimental.pallas import tpu as pltpu
from jax.sharding import PartitionSpec as P

HD = 64
BLOCK = 256
HEADS = 48
NB = 64
KMAX = 12
PAIR = 2 * HD
COLS = 64
SLICE = 32
PARTS = 3
NY = 8
AXES = ("tm", "head")
MASKED = -1e30
UNROLL = 4
QUADS = 4
STAGE_SHIFT = 6
STAGE_BASE = 1 << STAGE_SHIFT
LIST = NY * KMAX + UNROLL
EXP2_SCALE = 0.125 * 1.4426950408889634


def flat_index(x, y, z, core):
    return ((y * 2 + (x >> 1)) * 2 + core) * 16 + (x & 1) * 8 + z


COLUMN_GROUPS = [
    [flat_index(x, y, z, c) for y in range(8) for z in range(8)] for x in range(4) for c in range(2)
]


def moves(target):
    return [
        (flat_index(x, y, z, c), flat_index(target(x, c)[0], y, z, target(x, c)[1]))
        for x in range(4)
        for y in range(8)
        for z in range(8)
        for c in range(2)
    ]


SWAP_CORES = moves(lambda x, c: (x, 1 - c))
ONWARD = moves(lambda x, c: ((x + 1 - 2 * c) % 4, c))
ACROSS = moves(lambda x, c: ((x - 1 + 2 * c) % 4, 1 - c))


def low_lanes(shape):
    return lax.broadcasted_iota(jnp.int32, shape, len(shape) - 1) < HD


def swap_lanes(t):
    return jnp.concatenate([t[:, HD:], t[:, :HD]], axis=1)


def pack_kernel(q_hbm, k_hbm, v_hbm, out_hbm, q_ref, k_ref, v_ref, out_ref, in_sems, out_sems):
    half = SLICE // 2
    low, low_half = low_lanes((SLICE, PAIR)), low_lanes((half, PAIR))
    width, heads = HEADS * HD // PARTS, HEADS // PARTS
    reads, writes = [], []
    for part in range(PARTS):
        lanes = pl.ds(part * width, width)
        reads.append(
            [
                pltpu.make_async_copy(hbm.at[:, lanes], ref.at[:, lanes], in_sems.at[part, i])
                for i, (hbm, ref) in enumerate(((k_hbm, k_ref), (v_hbm, v_ref), (q_hbm, q_ref)))
            ]
        )
        for copy in reads[-1]:
            copy.start()

    def write(first, count):
        columns = pl.ds(first, count)
        copy = pltpu.make_async_copy(out_ref.at[columns], out_hbm.at[columns], out_sems.at[len(writes)])
        copy.start()
        writes.append(copy)

    out_ref[HEADS:] = jnp.zeros((COLS - HEADS, SLICE + half, PAIR), jnp.bfloat16)
    write(HEADS, COLS - HEADS)
    for part in range(PARTS):
        for copy in reads[part]:
            copy.wait()
        for even in range(part * heads, (part + 1) * heads, 2):
            lanes = pl.ds(even * HD, PAIR)
            k, v, q = k_ref[:, lanes], v_ref[:, lanes], q_ref[:, lanes]
            k_swap, v_swap, q_swap = (swap_lanes(t) for t in (k, v, q))
            out_ref[even, :SLICE, :] = jnp.where(low, k, v_swap)
            out_ref[even + 1, :SLICE, :] = jnp.where(low, k_swap, v)
            out_ref[even, SLICE:, :] = jnp.where(low_half, q[:half], q_swap[half:])
            out_ref[even + 1, SLICE:, :] = jnp.where(low_half, q_swap[:half], q[half:])
        write(part * heads, heads)
    for copy in writes:
        copy.wait()


def unpack_kernel(in_ref, out_hbm, out_ref, out_sems):
    half = SLICE // 2
    low = low_lanes((half, PAIR))
    width, heads = HEADS * HD // PARTS, HEADS // PARTS
    writes = []
    for part in range(PARTS):
        for even in range(part * heads, (part + 1) * heads, 2):
            lanes = pl.ds(even * HD, PAIR)
            first, second = in_ref[even], in_ref[even + 1]
            out_ref[:half, lanes] = jnp.where(low, first, swap_lanes(second))
            out_ref[half:, lanes] = jnp.where(low, swap_lanes(first), second)
        lanes = pl.ds(part * width, width)
        copy = pltpu.make_async_copy(out_ref.at[:, lanes], out_hbm.at[:, lanes], out_sems.at[part])
        copy.start()
        writes.append(copy)
    for copy in writes:
        copy.wait()


def list_pairs(order_ref, kept_ref, place_ref, where_is, pairs_ref, counts_ref):
    x_here, core_here, live = place_ref[0], place_ref[1], place_ref[2]

    def place(p, carry):
        away = (((p >> 2) & 1) * 2 + (p & 1) - x_here) & 3
        core = (p >> 1) & 1
        way = (away >> 1) ^ 1
        near = (way ^ core_here) * 2 + (core ^ way)
        near_at = jnp.where(near == 0, 2 * NY, STAGE_BASE + (near - 1) * NY)
        part = jnp.where((away & 1) == 1, near_at, away * STAGE_BASE + (core ^ core_here) * NY)
        where_is[order_ref[p]] = part + (p >> 3)
        return carry

    lax.fori_loop(0, NB, place, 0, unroll=8)

    def list_block(block, ends):
        p = block * NY + (x_here >> 1) * 4 + core_here * 2 + (x_here & 1)
        frame = order_ref[p]
        for j in range(KMAX):
            kept = kept_ref[j, frame]
            there = where_is[jnp.maximum(kept, 0)]
            stage = there >> STAGE_SHIFT
            end = jnp.where(stage == 0, ends[0], jnp.where(stage == 1, ends[1], ends[2]))
            pairs_ref[end] = block * STAGE_BASE + (there & (STAGE_BASE - 1))
            ends = tuple(
                e + ((kept >= 0) & (stage == k)).astype(jnp.int32) for k, e in enumerate(ends)
            )
        return ends

    starts = tuple(stage * LIST for stage in range(3))
    ends = lax.fori_loop(0, NY * live, list_block, tuple(jnp.int32(k) for k in starts))
    for stage in range(3):
        counts_ref[stage] = ends[stage] - starts[stage]
        for u in range(UNROLL):
            pairs_ref[ends[stage] + u] = NY * STAGE_BASE


def spread_queries(mine_ref, q_ref):
    half = SLICE // 2
    for block in range(NY):
        packed = mine_ref[pl.ds(block * NY, NY), SLICE:, :]
        low = low_lanes(packed.shape)
        swapped = jnp.concatenate([packed[:, :, HD:], packed[:, :, :HD]], axis=2)
        zero = jnp.zeros_like(packed)
        q = jnp.concatenate([jnp.where(low, packed, zero), jnp.where(low, swapped, zero)], axis=1)
        q_ref[block] = q.reshape(NY * 2 * half, PAIR)


def add_pairs(stage, pairs_ref, counts_ref, q_ref, kv, best_in, best, mixed_in, mixed, scores, top):
    quads = (counts_ref[stage] + 3) >> 2

    def each_pair(body):
        def run(first, n):
            for u in range(n):
                both = pairs_ref[stage * LIST + first + u]
                body(first + u, both >> STAGE_SHIFT, both & (STAGE_BASE - 1))

        @pl.loop(0, quads // QUADS)
        def _(t):
            run(t * QUADS * 4, QUADS * 4)

        left = quads % QUADS
        for some in range(1, QUADS):

            @pl.when(left == some)
            def _():
                run((quads - some) * 4, some * 4)

    if best_in is None:
        for block in range(NY):
            top[block] = jnp.full((BLOCK, PAIR), MASKED, jnp.float32)
            mixed[block] = jnp.zeros((BLOCK, PAIR), jnp.float32)
    else:
        for block in range(NY):
            top[block] = best_in[block]
    spare = jnp.zeros((BLOCK, PAIR), jnp.float32)
    top[NY], mixed[NY], best[NY] = spare, spare, spare

    def score(j, block, row):
        s = lax.dot_general(q_ref[block], kv[row], (((1,), (1,)), ((), ())), preferred_element_type=jnp.float32)
        scores[j] = s
        top[block] = jnp.maximum(top[block], jnp.maximum(s[:, :PAIR], s[:, PAIR:]))

    each_pair(score)

    for block in range(NY):
        new = jnp.broadcast_to(jnp.max(top[block], axis=1, keepdims=True), (BLOCK, PAIR))
        if best_in is not None:
            mixed[block] = mixed_in[block] * jnp.exp2((best_in[block] - new) * EXP2_SCALE)
        best[block] = new

    low = low_lanes((BLOCK, PAIR))

    def mix(j, block, row):
        peak = best[block]
        s = scores[j]
        weights = jnp.concatenate([s[:, :PAIR] - peak, s[:, PAIR:] - peak], axis=1)
        weights = jnp.exp2(weights * EXP2_SCALE).astype(jnp.bfloat16)
        values = jnp.where(low, jnp.ones((), jnp.bfloat16), kv[row])
        mixed[block] += jnp.dot(weights, values, preferred_element_type=jnp.float32)

    each_pair(mix)


def fetch(kv_refs, kv, sems):
    copies = [
        pltpu.make_async_copy(ref, kv.at[pl.ds(i * NY, NY)], sems.at[i]) for i, ref in enumerate(kv_refs)
    ]
    for copy in copies:
        copy.start()
    return copies


def plan_kernel(order_ref, kept_ref, place_ref, mine_ref, q_ref, pairs_ref, counts_ref, where_is):
    list_pairs(order_ref, kept_ref, place_ref, where_is, pairs_ref, counts_ref)
    spread_queries(mine_ref, q_ref)
    q_ref[NY] = jnp.zeros((BLOCK, PAIR), jnp.bfloat16)


def first_kernel(pairs_ref, counts_ref, q_ref, *refs):
    kv_refs = refs[:3]
    best, mixed, kv, scores, top, sems = refs[3:]
    for copy in fetch(kv_refs, kv, sems):
        copy.wait()
    add_pairs(0, pairs_ref, counts_ref, q_ref, kv, None, best, None, mixed, scores, top)


def second_kernel(pairs_ref, counts_ref, q_ref, best_in, mixed_in, *refs):
    kv_refs = refs[:3]
    best, mixed, kv, scores, top, sems = refs[3:]
    for copy in fetch(kv_refs, kv, sems):
        copy.wait()
    add_pairs(1, pairs_ref, counts_ref, q_ref, kv, best_in, best, mixed_in, mixed, scores, top)


def last_kernel(pairs_ref, counts_ref, q_ref, best_in, mixed_in, *refs):
    kv_refs = refs[:2]
    out_ref, best, mixed, kv, scores, top, sems = refs[2:]
    for copy in fetch(kv_refs, kv, sems):
        copy.wait()
    add_pairs(2, pairs_ref, counts_ref, q_ref, kv, best_in, best, mixed_in, mixed, scores, top)
    half = SLICE // 2
    low = low_lanes((NY, half, PAIR))
    for block in range(NY):
        here = mixed[block]
        there = jnp.concatenate([here[:, HD:], here[:, :HD]], axis=1).reshape(NY, SLICE, PAIR)
        here = here.reshape(NY, SLICE, PAIR)
        values = jnp.where(low, there[:, :half], here[:, half:])
        totals = jnp.where(low, here[:, :half], there[:, half:])
        out_ref[pl.ds(block * NY, NY)] = (values / totals).astype(jnp.bfloat16)


VMEM = pl.BlockSpec(memory_space=pltpu.VMEM)
SMEM = pl.BlockSpec(memory_space=pltpu.SMEM)
ANY = pl.BlockSpec(memory_space=pl.ANY)


def pack(q, k, v):
    rows = pltpu.VMEM((SLICE, HEADS * HD), jnp.bfloat16)
    packed = (COLS, SLICE + SLICE // 2, PAIR)
    return pl.pallas_call(
        pack_kernel,
        out_shape=jax.ShapeDtypeStruct(packed, jnp.bfloat16),
        in_specs=[ANY] * 3,
        out_specs=ANY,
        scratch_shapes=[
            rows,
            rows,
            rows,
            pltpu.VMEM(packed, jnp.bfloat16),
            pltpu.SemaphoreType.DMA((PARTS, 3)),
            pltpu.SemaphoreType.DMA((PARTS + 1,)),
        ],
        name="pack",
    )(q, k, v)


def unpack(mixed):
    return pl.pallas_call(
        unpack_kernel,
        out_shape=jax.ShapeDtypeStruct((SLICE, HEADS * HD), jnp.bfloat16),
        in_specs=[VMEM],
        out_specs=ANY,
        scratch_shapes=[
            pltpu.VMEM((SLICE, HEADS * HD), jnp.bfloat16),
            pltpu.SemaphoreType.DMA((PARTS,)),
        ],
        name="unpack",
    )(mixed)


STATE = jax.ShapeDtypeStruct((NY + 1, BLOCK, PAIR), jnp.float32)


def stage_scratch(chunks):
    return [
        pltpu.VMEM((chunks * NY, BLOCK, PAIR), jnp.bfloat16),
        pltpu.VMEM((NY * KMAX + UNROLL, BLOCK, BLOCK), jnp.float32),
        pltpu.VMEM((NY + 1, BLOCK, PAIR), jnp.float32),
    ]


def stage_options(share):
    return dict(
        compiler_params=pltpu.CompilerParams(vmem_limit_bytes=36 * 1024 * 1024),
        cost_estimate=pl.CostEstimate(flops=share, bytes_accessed=share, transcendentals=share),
    )


def plan(order, kept, place, mine):
    return pl.pallas_call(
        plan_kernel,
        out_shape=(
            jax.ShapeDtypeStruct((NY + 1, BLOCK, PAIR), jnp.bfloat16),
            jax.ShapeDtypeStruct((3 * LIST,), jnp.int32),
            jax.ShapeDtypeStruct((3,), jnp.int32),
        ),
        in_specs=[SMEM] * 3 + [VMEM],
        out_specs=(VMEM, SMEM, SMEM),
        scratch_shapes=[pltpu.SMEM((NB,), jnp.int32)],
        name="plan_pairs",
        **stage_options(1),
    )(order, kept, place, mine)


def attend_first(pairs, counts, q, early):
    return pl.pallas_call(
        first_kernel,
        out_shape=(STATE, STATE),
        in_specs=[SMEM] * 2 + [VMEM] + [ANY] * 3,
        out_specs=(VMEM, VMEM),
        scratch_shapes=stage_scratch(3) + [pltpu.SemaphoreType.DMA((3,))],
        name="attend_early",
        **stage_options(1),
    )(pairs, counts, q, *early)


def attend_second(pairs, counts, q, best, mixed, near):
    return pl.pallas_call(
        second_kernel,
        out_shape=(STATE, STATE),
        in_specs=[SMEM] * 2 + [VMEM] * 3 + [ANY] * 3,
        out_specs=(VMEM, VMEM),
        scratch_shapes=stage_scratch(3) + [pltpu.SemaphoreType.DMA((3,))],
        input_output_aliases={3: 0, 4: 1},
        name="attend_near",
        **stage_options(2),
    )(pairs, counts, q, best, mixed, *near)


def attend_last(pairs, counts, q, best, mixed, far):
    return pl.pallas_call(
        last_kernel,
        out_shape=jax.ShapeDtypeStruct((COLS, SLICE // 2, PAIR), jnp.bfloat16),
        in_specs=[SMEM] * 2 + [VMEM] * 3 + [ANY] * 2,
        out_specs=VMEM,
        scratch_shapes=[pltpu.VMEM((NY + 1, BLOCK, PAIR), jnp.float32)] * 2
        + stage_scratch(2)
        + [pltpu.SemaphoreType.DMA((2,))],
        name="attend_far",
        **stage_options(1),
    )(pairs, counts, q, best, mixed, *far)


def local(queries, key_vectors, value_vectors, frame_order, kept_blocks):
    tm, head = lax.axis_index("tm"), lax.axis_index("head")
    x_here = ((tm >> 1) & 1) * 2 + (head >> 3)
    column = (tm >> 2) * 8 + (head & 7)
    place = jnp.stack([x_here, tm & 1, (column < HEADS).astype(jnp.int32)]).astype(jnp.int32)
    packed = pack(queries, key_vectors, value_vectors)
    mine = lax.all_to_all(packed, AXES, 0, 0, tiled=True, axis_index_groups=COLUMN_GROUPS)
    kv = mine[:, :SLICE].reshape(NY, BLOCK, PAIR)
    swap = lambda t: lax.ppermute(t, AXES, SWAP_CORES)
    onward = lambda t: lax.ppermute(t, AXES, ONWARD)
    near_own = onward(kv)
    twin = swap(kv)
    q, pairs, counts = plan(frame_order, kept_blocks.T, place, mine)
    near_twin = lax.ppermute(kv, AXES, ACROSS)
    near_own, q = lax.optimization_barrier((near_own, q))
    far = onward(near_own)
    best, mixed = attend_first(pairs, counts, q, [kv, twin, near_own])
    near_own, best, mixed = lax.optimization_barrier((near_own, best, mixed))
    near = [near_twin, swap(near_own), swap(near_twin)]
    best, mixed = attend_second(pairs, counts, q, best, mixed, near)
    mixed = attend_last(pairs, counts, q, best, mixed, [far, swap(far)])
    back = lax.all_to_all(mixed, AXES, 0, 0, tiled=True, axis_index_groups=COLUMN_GROUPS)
    return unpack(back)


def solution(mesh):
    tokens = P(AXES, None)
    return jax.shard_map(
        local, mesh=mesh, in_specs=(tokens, tokens, tokens, P(), P()), out_specs=tokens, check_vma=False
    )
```

```python
import jax
import jax.numpy as jnp
from jax import lax
from jax.experimental import pallas as pl
from jax.experimental.pallas import tpu as pltpu
from jax.sharding import PartitionSpec as P

HD = 64
BLOCK = 256
HEADS = 48
NB = 64
KMAX = 12
PAIR = 2 * HD
COLS = 64
SLICE = 32
PARTS = 3
NY = 8
AXES = ("tm", "head")
MASKED = -1e30
UNROLL = 4
QUADS = 4
STAGE_SHIFT = 6
STAGE_BASE = 1 << STAGE_SHIFT
LIST = NY * KMAX + UNROLL
EXP2_SCALE = 0.125 * 1.4426950408889634


def flat_index(x, y, z, core):
    return ((y * 2 + (x >> 1)) * 2 + core) * 16 + (x & 1) * 8 + z


COLUMN_GROUPS = [
    [flat_index(x, y, z, c) for y in range(8) for z in range(8)] for x in range(4) for c in range(2)
]


def moves(target):
    return [
        (flat_index(x, y, z, c), flat_index(target(x, c)[0], y, z, target(x, c)[1]))
        for x in range(4)
        for y in range(8)
        for z in range(8)
        for c in range(2)
    ]


SWAP_CORES = moves(lambda x, c: (x, 1 - c))
ONWARD = moves(lambda x, c: ((x + 1 - 2 * c) % 4, c))
ACROSS = moves(lambda x, c: ((x - 1 + 2 * c) % 4, 1 - c))


def low_lanes(shape):
    return lax.broadcasted_iota(jnp.int32, shape, len(shape) - 1) < HD


def swap_lanes(t):
    return jnp.concatenate([t[:, HD:], t[:, :HD]], axis=1)


def pack_kernel(q_hbm, k_hbm, v_hbm, out_ref, q_ref, k_ref, v_ref, sems):
    half = SLICE // 2
    low, low_half = low_lanes((SLICE, PAIR)), low_lanes((half, PAIR))
    width, heads = HEADS * HD // PARTS, HEADS // PARTS
    reads = []
    for part in range(PARTS):
        lanes = pl.ds(part * width, width)
        for i, (hbm, ref) in enumerate(((k_hbm, k_ref), (v_hbm, v_ref), (q_hbm, q_ref))):
            reads.append(pltpu.make_async_copy(hbm.at[:, lanes], ref.at[:, lanes], sems.at[part, i]))
            reads[-1].start()
    out_ref[HEADS:] = jnp.zeros((COLS - HEADS, SLICE + half, PAIR), jnp.bfloat16)
    for part in range(PARTS):
        for copy in reads[3 * part : 3 * part + 3]:
            copy.wait()
        for even in range(part * heads, (part + 1) * heads, 2):
            lanes = pl.ds(even * HD, PAIR)
            k, v, q = k_ref[:, lanes], v_ref[:, lanes], q_ref[:, lanes]
            k_swap, v_swap, q_swap = (swap_lanes(t) for t in (k, v, q))
            out_ref[even, :SLICE, :] = jnp.where(low, k, v_swap)
            out_ref[even + 1, :SLICE, :] = jnp.where(low, k_swap, v)
            out_ref[even, SLICE:, :] = jnp.where(low_half, q[:half], q_swap[half:])
            out_ref[even + 1, SLICE:, :] = jnp.where(low_half, q_swap[:half], q[half:])


def unpack_kernel(in_ref, out_hbm, out_ref, out_sems):
    half = SLICE // 2
    low = low_lanes((half, PAIR))
    width, heads = HEADS * HD // PARTS, HEADS // PARTS
    writes = []
    for part in range(PARTS):
        for even in range(part * heads, (part + 1) * heads, 2):
            lanes = pl.ds(even * HD, PAIR)
            first, second = in_ref[even], in_ref[even + 1]
            out_ref[:half, lanes] = jnp.where(low, first, swap_lanes(second))
            out_ref[half:, lanes] = jnp.where(low, swap_lanes(first), second)
        lanes = pl.ds(part * width, width)
        copy = pltpu.make_async_copy(out_ref.at[:, lanes], out_hbm.at[:, lanes], out_sems.at[part])
        copy.start()
        writes.append(copy)
    for copy in writes:
        copy.wait()


def list_pairs(order_ref, kept_ref, place_ref, where_is, pairs_ref, counts_ref):
    x_here, core_here, live = place_ref[0], place_ref[1], place_ref[2]

    def place(p, carry):
        away = (((p >> 2) & 1) * 2 + (p & 1) - x_here) & 3
        core = (p >> 1) & 1
        way = (away >> 1) ^ 1
        near = (way ^ core_here) * 2 + (core ^ way)
        near_at = jnp.where(near == 0, 2 * NY, STAGE_BASE + (near - 1) * NY)
        part = jnp.where((away & 1) == 1, near_at, away * STAGE_BASE + (core ^ core_here) * NY)
        where_is[order_ref[p]] = part + (p >> 3)
        return carry

    lax.fori_loop(0, NB, place, 0, unroll=8)

    def list_block(block, ends):
        p = block * NY + (x_here >> 1) * 4 + core_here * 2 + (x_here & 1)
        frame = order_ref[p]
        for j in range(KMAX):
            kept = kept_ref[j, frame]
            there = where_is[jnp.maximum(kept, 0)]
            stage = there >> STAGE_SHIFT
            end = jnp.where(stage == 0, ends[0], jnp.where(stage == 1, ends[1], ends[2]))
            pairs_ref[end] = block * STAGE_BASE + (there & (STAGE_BASE - 1))
            ends = tuple(
                e + ((kept >= 0) & (stage == k)).astype(jnp.int32) for k, e in enumerate(ends)
            )
        return ends

    starts = tuple(stage * LIST for stage in range(3))
    ends = lax.fori_loop(0, NY * live, list_block, tuple(jnp.int32(k) for k in starts))
    for stage in range(3):
        counts_ref[stage] = ends[stage] - starts[stage]
        for u in range(UNROLL):
            pairs_ref[ends[stage] + u] = NY * STAGE_BASE


def spread_queries(mine_ref, q_ref):
    half = SLICE // 2
    for block in range(NY):
        packed = mine_ref[pl.ds(block * NY, NY), SLICE:, :]
        low = low_lanes(packed.shape)
        swapped = jnp.concatenate([packed[:, :, HD:], packed[:, :, :HD]], axis=2)
        zero = jnp.zeros_like(packed)
        q = jnp.concatenate([jnp.where(low, packed, zero), jnp.where(low, swapped, zero)], axis=1)
        q_ref[block] = q.reshape(NY * 2 * half, PAIR)


def add_pairs(stage, copies, pairs_ref, counts_ref, q_ref, kv, best_in, best, mixed_in, mixed, scores, top):
    quads = (counts_ref[stage] + 3) >> 2

    def each_pair(body):
        def run(first, n):
            for u in range(n):
                both = pairs_ref[stage * LIST + first + u]
                body(first + u, both >> STAGE_SHIFT, both & (STAGE_BASE - 1))

        @pl.loop(0, quads // QUADS)
        def _(t):
            run(t * QUADS * 4, QUADS * 4)

        left = quads % QUADS
        for some in range(1, QUADS):

            @pl.when(left == some)
            def _():
                run((quads - some) * 4, some * 4)

    if best_in is None:
        for block in range(NY):
            top[block] = jnp.full((BLOCK, PAIR), MASKED, jnp.float32)
            mixed[block] = jnp.zeros((BLOCK, PAIR), jnp.float32)
    else:
        for block in range(NY):
            top[block] = best_in[block]
    spare = jnp.zeros((BLOCK, PAIR), jnp.float32)
    top[NY], mixed[NY], best[NY] = spare, spare, spare
    for copy in copies:
        copy.wait()

    def score(j, block, row):
        s = lax.dot_general(q_ref[block], kv[row], (((1,), (1,)), ((), ())), preferred_element_type=jnp.float32)
        scores[j] = s
        top[block] = jnp.maximum(top[block], jnp.maximum(s[:, :PAIR], s[:, PAIR:]))

    each_pair(score)

    for block in range(NY):
        new = jnp.broadcast_to(jnp.max(top[block], axis=1, keepdims=True), (BLOCK, PAIR))
        if best_in is not None:
            mixed[block] = mixed_in[block] * jnp.exp2((best_in[block] - new) * EXP2_SCALE)
        best[block] = new

    low = low_lanes((BLOCK, PAIR))

    def mix(j, block, row):
        peak = best[block]
        s = scores[j]
        weights = jnp.concatenate([s[:, :PAIR] - peak, s[:, PAIR:] - peak], axis=1)
        weights = jnp.exp2(weights * EXP2_SCALE).astype(jnp.bfloat16)
        values = jnp.where(low, jnp.ones((), jnp.bfloat16), kv[row])
        mixed[block] += jnp.dot(weights, values, preferred_element_type=jnp.float32)

    each_pair(mix)


def fetch(kv_refs, kv, sems):
    copies = [
        pltpu.make_async_copy(ref, kv.at[pl.ds(i * NY, NY)], sems.at[i]) for i, ref in enumerate(kv_refs)
    ]
    for copy in copies:
        copy.start()
    return copies


def plan_kernel(order_ref, kept_ref, place_ref, mine_ref, q_ref, pairs_ref, counts_ref, where_is):
    list_pairs(order_ref, kept_ref, place_ref, where_is, pairs_ref, counts_ref)
    spread_queries(mine_ref, q_ref)
    q_ref[NY] = jnp.zeros((BLOCK, PAIR), jnp.bfloat16)


def first_kernel(pairs_ref, counts_ref, q_ref, *refs):
    kv_refs = refs[:3]
    best, mixed, kv, scores, top, sems = refs[3:]
    copies = fetch(kv_refs, kv, sems)
    add_pairs(0, copies, pairs_ref, counts_ref, q_ref, kv, None, best, None, mixed, scores, top)


def second_kernel(pairs_ref, counts_ref, q_ref, best_in, mixed_in, *refs):
    kv_refs = refs[:3]
    best, mixed, kv, scores, top, sems = refs[3:]
    copies = fetch(kv_refs, kv, sems)
    add_pairs(1, copies, pairs_ref, counts_ref, q_ref, kv, best_in, best, mixed_in, mixed, scores, top)


def last_kernel(pairs_ref, counts_ref, q_ref, best_in, mixed_in, *refs):
    kv_refs = refs[:2]
    out_ref, best, mixed, kv, scores, top, sems = refs[2:]
    copies = fetch(kv_refs, kv, sems)
    add_pairs(2, copies, pairs_ref, counts_ref, q_ref, kv, best_in, best, mixed_in, mixed, scores, top)
    half = SLICE // 2
    low = low_lanes((NY, half, PAIR))
    for block in range(NY):
        here = mixed[block]
        there = jnp.concatenate([here[:, HD:], here[:, :HD]], axis=1).reshape(NY, SLICE, PAIR)
        here = here.reshape(NY, SLICE, PAIR)
        values = jnp.where(low, there[:, :half], here[:, half:])
        totals = jnp.where(low, here[:, :half], there[:, half:])
        out_ref[pl.ds(block * NY, NY)] = (values / totals).astype(jnp.bfloat16)


VMEM = pl.BlockSpec(memory_space=pltpu.VMEM)
SMEM = pl.BlockSpec(memory_space=pltpu.SMEM)
ANY = pl.BlockSpec(memory_space=pl.ANY)


def pack(q, k, v):
    rows = pltpu.VMEM((SLICE, HEADS * HD), jnp.bfloat16)
    return pl.pallas_call(
        pack_kernel,
        out_shape=pltpu.VMEM((COLS, SLICE + SLICE // 2, PAIR), jnp.bfloat16),
        in_specs=[ANY] * 3,
        out_specs=VMEM,
        scratch_shapes=[rows, rows, rows, pltpu.SemaphoreType.DMA((PARTS, 3))],
        name="pack",
    )(q, k, v)


def unpack(mixed):
    return pl.pallas_call(
        unpack_kernel,
        out_shape=jax.ShapeDtypeStruct((SLICE, HEADS * HD), jnp.bfloat16),
        in_specs=[VMEM],
        out_specs=ANY,
        scratch_shapes=[
            pltpu.VMEM((SLICE, HEADS * HD), jnp.bfloat16),
            pltpu.SemaphoreType.DMA((PARTS,)),
        ],
        name="unpack",
    )(mixed)


STATE = jax.ShapeDtypeStruct((NY + 1, BLOCK, PAIR), jnp.float32)


def stage_scratch(chunks):
    return [
        pltpu.VMEM((chunks * NY, BLOCK, PAIR), jnp.bfloat16),
        pltpu.VMEM((NY * KMAX + UNROLL, BLOCK, BLOCK), jnp.float32),
        pltpu.VMEM((NY + 1, BLOCK, PAIR), jnp.float32),
    ]


def stage_options(share):
    return dict(
        compiler_params=pltpu.CompilerParams(vmem_limit_bytes=36 * 1024 * 1024),
        cost_estimate=pl.CostEstimate(flops=share, bytes_accessed=share, transcendentals=share),
    )


def plan(order, kept, place, mine):
    return pl.pallas_call(
        plan_kernel,
        out_shape=(
            jax.ShapeDtypeStruct((NY + 1, BLOCK, PAIR), jnp.bfloat16),
            pltpu.SMEM((3 * LIST,), jnp.int32),
            pltpu.SMEM((3,), jnp.int32),
        ),
        in_specs=[SMEM] * 3 + [VMEM],
        out_specs=(VMEM, SMEM, SMEM),
        scratch_shapes=[pltpu.SMEM((NB,), jnp.int32)],
        name="plan_pairs",
        **stage_options(1),
    )(order, kept, place, mine)


def attend_first(pairs, counts, q, early):
    return pl.pallas_call(
        first_kernel,
        out_shape=(STATE, STATE),
        in_specs=[SMEM] * 2 + [VMEM] + [ANY] * 3,
        out_specs=(VMEM, VMEM),
        scratch_shapes=stage_scratch(3) + [pltpu.SemaphoreType.DMA((3,))],
        name="attend_early",
        **stage_options(1),
    )(pairs, counts, q, *early)


def attend_second(pairs, counts, q, best, mixed, near):
    return pl.pallas_call(
        second_kernel,
        out_shape=(STATE, STATE),
        in_specs=[SMEM] * 2 + [VMEM] * 3 + [ANY] * 3,
        out_specs=(VMEM, VMEM),
        scratch_shapes=stage_scratch(3) + [pltpu.SemaphoreType.DMA((3,))],
        input_output_aliases={3: 0, 4: 1},
        name="attend_near",
        **stage_options(2),
    )(pairs, counts, q, best, mixed, *near)


def attend_last(pairs, counts, q, best, mixed, far):
    return pl.pallas_call(
        last_kernel,
        out_shape=jax.ShapeDtypeStruct((COLS, SLICE // 2, PAIR), jnp.bfloat16),
        in_specs=[SMEM] * 2 + [VMEM] * 3 + [ANY] * 2,
        out_specs=VMEM,
        scratch_shapes=[pltpu.VMEM((NY + 1, BLOCK, PAIR), jnp.float32)] * 2
        + stage_scratch(2)
        + [pltpu.SemaphoreType.DMA((2,))],
        name="attend_far",
        **stage_options(1),
    )(pairs, counts, q, best, mixed, *far)


def local(queries, key_vectors, value_vectors, frame_order, kept_blocks):
    tm, head = lax.axis_index("tm"), lax.axis_index("head")
    x_here = ((tm >> 1) & 1) * 2 + (head >> 3)
    column = (tm >> 2) * 8 + (head & 7)
    place = jnp.stack([x_here, tm & 1, (column < HEADS).astype(jnp.int32)]).astype(jnp.int32)
    packed = pack(queries, key_vectors, value_vectors)
    mine = lax.all_to_all(packed, AXES, 0, 0, tiled=True, axis_index_groups=COLUMN_GROUPS)
    kv = mine[:, :SLICE].reshape(NY, BLOCK, PAIR)
    swap = lambda t: lax.ppermute(t, AXES, SWAP_CORES)
    onward = lambda t: lax.ppermute(t, AXES, ONWARD)
    near_own = onward(kv)
    twin = swap(kv)
    q, pairs, counts = plan(frame_order, kept_blocks.T, place, mine)
    near_twin = lax.ppermute(kv, AXES, ACROSS)
    near_own, q = lax.optimization_barrier((near_own, q))
    far = onward(near_own)
    best, mixed = attend_first(pairs, counts, q, [kv, twin, near_own])
    near_own, best, mixed = lax.optimization_barrier((near_own, best, mixed))
    near = [near_twin, swap(near_own), swap(near_twin)]
    best, mixed = attend_second(pairs, counts, q, best, mixed, near)
    mixed = attend_last(pairs, counts, q, best, mixed, [far, swap(far)])
    back = lax.all_to_all(mixed, AXES, 0, 0, tiled=True, axis_index_groups=COLUMN_GROUPS)
    return unpack(pltpu.with_memory_space_constraint(back, pltpu.VMEM))


def solution(mesh):
    tokens = P(AXES, None)
    return jax.shard_map(
        local, mesh=mesh, in_specs=(tokens, tokens, tokens, P(), P()), out_specs=tokens, check_vma=False
    )
```

```python
import jax
import jax.numpy as jnp
from jax import lax
from jax.experimental import pallas as pl
from jax.experimental.pallas import tpu as pltpu
from jax.sharding import PartitionSpec as P

HD = 64
BLOCK = 256
HEADS = 48
NB = 64
KMAX = 12
PAIR = 2 * HD
COLS = 64
SLICE = 32
PARTS = 3
NY = 8
AXES = ("tm", "head")
MASKED = -1e30
UNROLL = 4
QUADS = 4
STAGE_SHIFT = 6
STAGE_BASE = 1 << STAGE_SHIFT
LIST = NY * KMAX + UNROLL
EXP2_SCALE = 0.125 * 1.4426950408889634


def flat_index(x, y, z, core):
    return ((y * 2 + (x >> 1)) * 2 + core) * 16 + (x & 1) * 8 + z


COLUMN_GROUPS = [
    [flat_index(x, y, z, c) for y in range(8) for z in range(8)] for x in range(4) for c in range(2)
]


def moves(target):
    return [
        (flat_index(x, y, z, c), flat_index(target(x, c)[0], y, z, target(x, c)[1]))
        for x in range(4)
        for y in range(8)
        for z in range(8)
        for c in range(2)
    ]


SWAP_CORES = moves(lambda x, c: (x, 1 - c))
ONWARD = moves(lambda x, c: ((x + 1 - 2 * c) % 4, c))
ACROSS = moves(lambda x, c: ((x - 1 + 2 * c) % 4, 1 - c))


def low_lanes(shape):
    return lax.broadcasted_iota(jnp.int32, shape, len(shape) - 1) < HD


def swap_lanes(t):
    return jnp.concatenate([t[:, HD:], t[:, :HD]], axis=1)


def pack_kernel(q_hbm, k_hbm, v_hbm, out_ref, q_ref, k_ref, v_ref, sems):
    half = SLICE // 2
    low, low_half = low_lanes((SLICE, PAIR)), low_lanes((half, PAIR))
    width, heads = HEADS * HD // PARTS, HEADS // PARTS
    reads = []
    for part in range(PARTS):
        lanes = pl.ds(part * width, width)
        for i, (hbm, ref) in enumerate(((k_hbm, k_ref), (v_hbm, v_ref), (q_hbm, q_ref))):
            reads.append(pltpu.make_async_copy(hbm.at[:, lanes], ref.at[:, lanes], sems.at[part, i]))
            reads[-1].start()
    out_ref[HEADS:] = jnp.zeros((COLS - HEADS, SLICE + half, PAIR), jnp.bfloat16)
    for part in range(PARTS):
        for copy in reads[3 * part : 3 * part + 3]:
            copy.wait()
        for even in range(part * heads, (part + 1) * heads, 2):
            lanes = pl.ds(even * HD, PAIR)
            k, v, q = k_ref[:, lanes], v_ref[:, lanes], q_ref[:, lanes]
            k_swap, v_swap, q_swap = (swap_lanes(t) for t in (k, v, q))
            out_ref[even, :SLICE, :] = jnp.where(low, k, v_swap)
            out_ref[even + 1, :SLICE, :] = jnp.where(low, k_swap, v)
            out_ref[even, SLICE:, :] = jnp.where(low_half, q[:half], q_swap[half:])
            out_ref[even + 1, SLICE:, :] = jnp.where(low_half, q_swap[:half], q[half:])


def unpack_kernel(in_ref, out_hbm, out_ref, out_sems):
    half = SLICE // 2
    low = low_lanes((half, PAIR))
    width, heads = HEADS * HD // PARTS, HEADS // PARTS
    writes = []
    for part in range(PARTS):
        for even in range(part * heads, (part + 1) * heads, 2):
            lanes = pl.ds(even * HD, PAIR)
            first, second = in_ref[even], in_ref[even + 1]
            out_ref[:half, lanes] = jnp.where(low, first, swap_lanes(second))
            out_ref[half:, lanes] = jnp.where(low, swap_lanes(first), second)
        lanes = pl.ds(part * width, width)
        copy = pltpu.make_async_copy(out_ref.at[:, lanes], out_hbm.at[:, lanes], out_sems.at[part])
        copy.start()
        writes.append(copy)
    for copy in writes:
        copy.wait()


def list_pairs(order_ref, kept_ref, place_ref, where_is, pairs_ref, counts_ref):
    x_here, core_here, live = place_ref[0], place_ref[1], place_ref[2]

    def place(p, carry):
        away = (((p >> 2) & 1) * 2 + (p & 1) - x_here) & 3
        core = (p >> 1) & 1
        way = (away >> 1) ^ 1
        near = (way ^ core_here) * 2 + (core ^ way)
        near_at = jnp.where(near == 0, 2 * NY, STAGE_BASE + (near - 1) * NY)
        part = jnp.where((away & 1) == 1, near_at, away * STAGE_BASE + (core ^ core_here) * NY)
        where_is[order_ref[p]] = part + (p >> 3)
        return carry

    lax.fori_loop(0, NB, place, 0, unroll=8)

    def list_block(block, ends):
        p = block * NY + (x_here >> 1) * 4 + core_here * 2 + (x_here & 1)
        frame = order_ref[p]
        for j in range(KMAX):
            kept = kept_ref[j, frame]
            there = where_is[jnp.maximum(kept, 0)]
            stage = there >> STAGE_SHIFT
            end = jnp.where(stage == 0, ends[0], jnp.where(stage == 1, ends[1], ends[2]))
            pairs_ref[end] = block * STAGE_BASE + (there & (STAGE_BASE - 1))
            ends = tuple(
                e + ((kept >= 0) & (stage == k)).astype(jnp.int32) for k, e in enumerate(ends)
            )
        return ends

    starts = tuple(stage * LIST for stage in range(3))
    ends = lax.fori_loop(0, NY * live, list_block, tuple(jnp.int32(k) for k in starts))
    for stage in range(3):
        counts_ref[stage] = ends[stage] - starts[stage]
        for u in range(UNROLL):
            pairs_ref[ends[stage] + u] = NY * STAGE_BASE


def spread_queries(mine_ref, q_ref):
    half = SLICE // 2
    for block in range(NY):
        packed = mine_ref[pl.ds(block * NY, NY), SLICE:, :]
        low = low_lanes(packed.shape)
        swapped = jnp.concatenate([packed[:, :, HD:], packed[:, :, :HD]], axis=2)
        zero = jnp.zeros_like(packed)
        q = jnp.concatenate([jnp.where(low, packed, zero), jnp.where(low, swapped, zero)], axis=1)
        q_ref[block] = q.reshape(NY * 2 * half, PAIR)


def add_pairs(stage, copies, pairs_ref, counts_ref, q_ref, kv, best_in, best, mixed_in, mixed, scores, top):
    quads = (counts_ref[stage] + 3) >> 2

    def each_pair(body):
        def run(first, n):
            for u in range(n):
                both = pairs_ref[stage * LIST + first + u]
                body(first + u, both >> STAGE_SHIFT, both & (STAGE_BASE - 1))

        @pl.loop(0, quads // QUADS)
        def _(t):
            run(t * QUADS * 4, QUADS * 4)

        for some in (2, 1):

            @pl.when((quads & some) != 0)
            def _():
                run((quads & (-2 * some)) * 4, some * 4)

    if best_in is None:
        for block in range(NY):
            top[block] = jnp.full((BLOCK, PAIR), MASKED, jnp.float32)
            mixed[block] = jnp.zeros((BLOCK, PAIR), jnp.float32)
    else:
        for block in range(NY):
            top[block] = best_in[block]
    spare = jnp.zeros((BLOCK, PAIR), jnp.float32)
    top[NY], mixed[NY], best[NY] = spare, spare, spare
    for copy in copies:
        copy.wait()

    def score(j, block, row):
        s = lax.dot_general(q_ref[block], kv[row], (((1,), (1,)), ((), ())), preferred_element_type=jnp.float32)
        scores[j] = s
        top[block] = jnp.maximum(top[block], jnp.maximum(s[:, :PAIR], s[:, PAIR:]))

    each_pair(score)

    for block in range(NY):
        new = jnp.broadcast_to(jnp.max(top[block], axis=1, keepdims=True), (BLOCK, PAIR))
        if best_in is not None:
            mixed[block] = mixed_in[block] * jnp.exp2((best_in[block] - new) * EXP2_SCALE)
        best[block] = new

    low = low_lanes((BLOCK, PAIR))

    def mix(j, block, row):
        peak = best[block]
        s = scores[j]
        weights = jnp.concatenate([s[:, :PAIR] - peak, s[:, PAIR:] - peak], axis=1)
        weights = jnp.exp2(weights * EXP2_SCALE).astype(jnp.bfloat16)
        values = jnp.where(low, jnp.ones((), jnp.bfloat16), kv[row])
        mixed[block] += jnp.dot(weights, values, preferred_element_type=jnp.float32)

    each_pair(mix)


def fetch(kv_refs, kv, sems):
    copies = [
        pltpu.make_async_copy(ref, kv.at[pl.ds(i * NY, NY)], sems.at[i]) for i, ref in enumerate(kv_refs)
    ]
    for copy in copies:
        copy.start()
    return copies


def plan_kernel(order_ref, kept_ref, place_ref, mine_ref, q_ref, pairs_ref, counts_ref, where_is):
    list_pairs(order_ref, kept_ref, place_ref, where_is, pairs_ref, counts_ref)
    spread_queries(mine_ref, q_ref)
    q_ref[NY] = jnp.zeros((BLOCK, PAIR), jnp.bfloat16)


def first_kernel(pairs_ref, counts_ref, q_ref, *refs):
    kv_refs = refs[:3]
    best, mixed, kv, scores, top, sems = refs[3:]
    copies = fetch(kv_refs, kv, sems)
    add_pairs(0, copies, pairs_ref, counts_ref, q_ref, kv, None, best, None, mixed, scores, top)


def second_kernel(pairs_ref, counts_ref, q_ref, best_in, mixed_in, *refs):
    kv_refs = refs[:3]
    best, mixed, kv, scores, top, sems = refs[3:]
    copies = fetch(kv_refs, kv, sems)
    add_pairs(1, copies, pairs_ref, counts_ref, q_ref, kv, best_in, best, mixed_in, mixed, scores, top)


def last_kernel(pairs_ref, counts_ref, q_ref, best_in, mixed_in, *refs):
    kv_refs = refs[:2]
    out_ref, best, mixed, kv, scores, top, sems = refs[2:]
    copies = fetch(kv_refs, kv, sems)
    add_pairs(2, copies, pairs_ref, counts_ref, q_ref, kv, best_in, best, mixed_in, mixed, scores, top)
    half = SLICE // 2
    low = low_lanes((NY, half, PAIR))
    for block in range(NY):
        here = mixed[block]
        there = jnp.concatenate([here[:, HD:], here[:, :HD]], axis=1).reshape(NY, SLICE, PAIR)
        here = here.reshape(NY, SLICE, PAIR)
        values = jnp.where(low, there[:, :half], here[:, half:])
        totals = jnp.where(low, here[:, :half], there[:, half:])
        out_ref[pl.ds(block * NY, NY)] = (values / totals).astype(jnp.bfloat16)


VMEM = pl.BlockSpec(memory_space=pltpu.VMEM)
SMEM = pl.BlockSpec(memory_space=pltpu.SMEM)
ANY = pl.BlockSpec(memory_space=pl.ANY)


def pack(q, k, v):
    rows = pltpu.VMEM((SLICE, HEADS * HD), jnp.bfloat16)
    return pl.pallas_call(
        pack_kernel,
        out_shape=pltpu.VMEM((COLS, SLICE + SLICE // 2, PAIR), jnp.bfloat16),
        in_specs=[ANY] * 3,
        out_specs=VMEM,
        scratch_shapes=[rows, rows, rows, pltpu.SemaphoreType.DMA((PARTS, 3))],
        name="pack",
    )(q, k, v)


def unpack(mixed):
    return pl.pallas_call(
        unpack_kernel,
        out_shape=jax.ShapeDtypeStruct((SLICE, HEADS * HD), jnp.bfloat16),
        in_specs=[VMEM],
        out_specs=ANY,
        scratch_shapes=[
            pltpu.VMEM((SLICE, HEADS * HD), jnp.bfloat16),
            pltpu.SemaphoreType.DMA((PARTS,)),
        ],
        name="unpack",
    )(mixed)


STATE = jax.ShapeDtypeStruct((NY + 1, BLOCK, PAIR), jnp.float32)


def stage_scratch(chunks):
    return [
        pltpu.VMEM((chunks * NY, BLOCK, PAIR), jnp.bfloat16),
        pltpu.VMEM((NY * KMAX + UNROLL, BLOCK, BLOCK), jnp.float32),
        pltpu.VMEM((NY + 1, BLOCK, PAIR), jnp.float32),
    ]


def stage_options(share):
    return dict(
        compiler_params=pltpu.CompilerParams(vmem_limit_bytes=36 * 1024 * 1024),
        cost_estimate=pl.CostEstimate(flops=share, bytes_accessed=share, transcendentals=share),
    )


def plan(order, kept, place, mine):
    return pl.pallas_call(
        plan_kernel,
        out_shape=(
            jax.ShapeDtypeStruct((NY + 1, BLOCK, PAIR), jnp.bfloat16),
            pltpu.SMEM((3 * LIST,), jnp.int32),
            pltpu.SMEM((3,), jnp.int32),
        ),
        in_specs=[SMEM] * 3 + [VMEM],
        out_specs=(VMEM, SMEM, SMEM),
        scratch_shapes=[pltpu.SMEM((NB,), jnp.int32)],
        name="plan_pairs",
        **stage_options(1),
    )(order, kept, place, mine)


def attend_first(pairs, counts, q, early):
    return pl.pallas_call(
        first_kernel,
        out_shape=(STATE, STATE),
        in_specs=[SMEM] * 2 + [VMEM] + [ANY] * 3,
        out_specs=(VMEM, VMEM),
        scratch_shapes=stage_scratch(3) + [pltpu.SemaphoreType.DMA((3,))],
        name="attend_early",
        **stage_options(1),
    )(pairs, counts, q, *early)


def attend_second(pairs, counts, q, best, mixed, near):
    return pl.pallas_call(
        second_kernel,
        out_shape=(STATE, STATE),
        in_specs=[SMEM] * 2 + [VMEM] * 3 + [ANY] * 3,
        out_specs=(VMEM, VMEM),
        scratch_shapes=stage_scratch(3) + [pltpu.SemaphoreType.DMA((3,))],
        input_output_aliases={3: 0, 4: 1},
        name="attend_near",
        **stage_options(2),
    )(pairs, counts, q, best, mixed, *near)


def attend_last(pairs, counts, q, best, mixed, far):
    return pl.pallas_call(
        last_kernel,
        out_shape=jax.ShapeDtypeStruct((COLS, SLICE // 2, PAIR), jnp.bfloat16),
        in_specs=[SMEM] * 2 + [VMEM] * 3 + [ANY] * 2,
        out_specs=VMEM,
        scratch_shapes=[pltpu.VMEM((NY + 1, BLOCK, PAIR), jnp.float32)] * 2
        + stage_scratch(2)
        + [pltpu.SemaphoreType.DMA((2,))],
        name="attend_far",
        **stage_options(1),
    )(pairs, counts, q, best, mixed, *far)


def local(queries, key_vectors, value_vectors, frame_order, kept_blocks):
    tm, head = lax.axis_index("tm"), lax.axis_index("head")
    x_here = ((tm >> 1) & 1) * 2 + (head >> 3)
    column = (tm >> 2) * 8 + (head & 7)
    place = jnp.stack([x_here, tm & 1, (column < HEADS).astype(jnp.int32)]).astype(jnp.int32)
    packed = pack(queries, key_vectors, value_vectors)
    mine = lax.all_to_all(packed, AXES, 0, 0, tiled=True, axis_index_groups=COLUMN_GROUPS)
    kv = mine[:, :SLICE].reshape(NY, BLOCK, PAIR)
    swap = lambda t: lax.ppermute(t, AXES, SWAP_CORES)
    onward = lambda t: lax.ppermute(t, AXES, ONWARD)
    near_own = onward(kv)
    twin = swap(kv)
    q, pairs, counts = plan(frame_order, kept_blocks.T, place, mine)
    near_twin = lax.ppermute(kv, AXES, ACROSS)
    near_own, q = lax.optimization_barrier((near_own, q))
    far = onward(near_own)
    best, mixed = attend_first(pairs, counts, q, [kv, twin, near_own])
    near_own, best, mixed = lax.optimization_barrier((near_own, best, mixed))
    near = [near_twin, swap(near_own), swap(near_twin)]
    best, mixed = attend_second(pairs, counts, q, best, mixed, near)
    mixed = attend_last(pairs, counts, q, best, mixed, [far, swap(far)])
    back = lax.all_to_all(mixed, AXES, 0, 0, tiled=True, axis_index_groups=COLUMN_GROUPS)
    return unpack(pltpu.with_memory_space_constraint(back, pltpu.VMEM))


def solution(mesh):
    tokens = P(AXES, None)
    return jax.shard_map(
        local, mesh=mesh, in_specs=(tokens, tokens, tokens, P(), P()), out_specs=tokens, check_vma=False
    )
```

```python
import jax
import jax.numpy as jnp
from jax import lax
from jax.experimental import pallas as pl
from jax.experimental.pallas import tpu as pltpu
from jax.sharding import PartitionSpec as P

HD = 64
BLOCK = 256
HEADS = 48
NB = 64
KMAX = 12
PAIR = 2 * HD
COLS = 64
SLICE = 32
PARTS = 2
NY = 8
AXES = ("tm", "head")
MASKED = -1e30
UNROLL = 4
QUADS = 4
STAGE_SHIFT = 6
STAGE_BASE = 1 << STAGE_SHIFT
LIST = NY * KMAX + UNROLL
EXP2_SCALE = 0.125 * 1.4426950408889634


def flat_index(x, y, z, core):
    return ((y * 2 + (x >> 1)) * 2 + core) * 16 + (x & 1) * 8 + z


COLUMN_GROUPS = [
    [flat_index(x, y, z, c) for y in range(8) for z in range(8)] for x in range(4) for c in range(2)
]


def moves(target):
    return [
        (flat_index(x, y, z, c), flat_index(target(x, c)[0], y, z, target(x, c)[1]))
        for x in range(4)
        for y in range(8)
        for z in range(8)
        for c in range(2)
    ]


SWAP_CORES = moves(lambda x, c: (x, 1 - c))
ONWARD = moves(lambda x, c: ((x + 1 - 2 * c) % 4, c))
ACROSS = moves(lambda x, c: ((x - 1 + 2 * c) % 4, 1 - c))


def low_lanes(shape):
    return lax.broadcasted_iota(jnp.int32, shape, len(shape) - 1) < HD


def swap_lanes(t):
    return jnp.concatenate([t[:, HD:], t[:, :HD]], axis=1)


def pack_kernel(q_hbm, k_hbm, v_hbm, out_ref, q_ref, k_ref, v_ref, sems):
    half = SLICE // 2
    low, low_half = low_lanes((SLICE, PAIR)), low_lanes((half, PAIR))
    width, heads = HEADS * HD // PARTS, HEADS // PARTS
    reads = []
    for part in range(PARTS):
        lanes = pl.ds(part * width, width)
        for i, (hbm, ref) in enumerate(((k_hbm, k_ref), (v_hbm, v_ref), (q_hbm, q_ref))):
            reads.append(pltpu.make_async_copy(hbm.at[:, lanes], ref.at[:, lanes], sems.at[part, i]))
            reads[-1].start()
    out_ref[HEADS:] = jnp.zeros((COLS - HEADS, SLICE + half, PAIR), jnp.bfloat16)
    for part in range(PARTS):
        for copy in reads[3 * part : 3 * part + 3]:
            copy.wait()
        for even in range(part * heads, (part + 1) * heads, 2):
            lanes = pl.ds(even * HD, PAIR)
            k, v, q = k_ref[:, lanes], v_ref[:, lanes], q_ref[:, lanes]
            k_swap, v_swap, q_swap = (swap_lanes(t) for t in (k, v, q))
            out_ref[even, :SLICE, :] = jnp.where(low, k, v_swap)
            out_ref[even + 1, :SLICE, :] = jnp.where(low, k_swap, v)
            out_ref[even, SLICE:, :] = jnp.where(low_half, q[:half], q_swap[half:])
            out_ref[even + 1, SLICE:, :] = jnp.where(low_half, q_swap[:half], q[half:])


def unpack_kernel(in_ref, out_hbm, out_ref, out_sems):
    half = SLICE // 2
    low = low_lanes((half, PAIR))
    width, heads = HEADS * HD // PARTS, HEADS // PARTS
    writes = []
    for part in range(PARTS):
        for even in range(part * heads, (part + 1) * heads, 2):
            lanes = pl.ds(even * HD, PAIR)
            first, second = in_ref[even], in_ref[even + 1]
            out_ref[:half, lanes] = jnp.where(low, first, swap_lanes(second))
            out_ref[half:, lanes] = jnp.where(low, swap_lanes(first), second)
        lanes = pl.ds(part * width, width)
        copy = pltpu.make_async_copy(out_ref.at[:, lanes], out_hbm.at[:, lanes], out_sems.at[part])
        copy.start()
        writes.append(copy)
    for copy in writes:
        copy.wait()


def list_pairs(order_ref, kept_ref, place_ref, where_is, pairs_ref, counts_ref):
    x_here, core_here, live = place_ref[0], place_ref[1], place_ref[2]

    def place(p, carry):
        away = (((p >> 2) & 1) * 2 + (p & 1) - x_here) & 3
        core = (p >> 1) & 1
        way = (away >> 1) ^ 1
        near = (way ^ core_here) * 2 + (core ^ way)
        near_at = jnp.where(near == 0, 2 * NY, STAGE_BASE + (near - 1) * NY)
        part = jnp.where((away & 1) == 1, near_at, away * STAGE_BASE + (core ^ core_here) * NY)
        where_is[order_ref[p]] = part + (p >> 3)
        return carry

    lax.fori_loop(0, NB, place, 0, unroll=8)

    def list_block(block, ends):
        p = block * NY + (x_here >> 1) * 4 + core_here * 2 + (x_here & 1)
        frame = order_ref[p]
        for j in range(KMAX):
            kept = kept_ref[j, frame]
            there = where_is[jnp.maximum(kept, 0)]
            stage = there >> STAGE_SHIFT
            end = jnp.where(stage == 0, ends[0], jnp.where(stage == 1, ends[1], ends[2]))
            pairs_ref[end] = block * STAGE_BASE + (there & (STAGE_BASE - 1))
            ends = tuple(
                e + ((kept >= 0) & (stage == k)).astype(jnp.int32) for k, e in enumerate(ends)
            )
        return ends

    starts = tuple(stage * LIST for stage in range(3))
    ends = lax.fori_loop(0, NY * live, list_block, tuple(jnp.int32(k) for k in starts))
    for stage in range(3):
        counts_ref[stage] = ends[stage] - starts[stage]
        for u in range(UNROLL):
            pairs_ref[ends[stage] + u] = NY * STAGE_BASE


def spread_queries(mine_ref, q_ref):
    half = SLICE // 2
    for block in range(NY):
        packed = mine_ref[pl.ds(block * NY, NY), SLICE:, :]
        low = low_lanes(packed.shape)
        swapped = jnp.concatenate([packed[:, :, HD:], packed[:, :, :HD]], axis=2)
        zero = jnp.zeros_like(packed)
        q = jnp.concatenate([jnp.where(low, packed, zero), jnp.where(low, swapped, zero)], axis=1)
        q_ref[block] = q.reshape(NY * 2 * half, PAIR)


def add_pairs(stage, copies, pairs_ref, counts_ref, q_ref, kv, best_in, best, mixed_in, mixed, scores, top):
    quads = (counts_ref[stage] + 3) >> 2

    def each_pair(body):
        def run(first, n):
            for u in range(n):
                both = pairs_ref[stage * LIST + first + u]
                body(first + u, both >> STAGE_SHIFT, both & (STAGE_BASE - 1))

        @pl.loop(0, quads // QUADS)
        def _(t):
            run(t * QUADS * 4, QUADS * 4)

        for some in (2, 1):

            @pl.when((quads & some) != 0)
            def _():
                run((quads & (-2 * some)) * 4, some * 4)

    if best_in is None:
        for block in range(NY):
            top[block] = jnp.full((BLOCK, PAIR), MASKED, jnp.float32)
            mixed[block] = jnp.zeros((BLOCK, PAIR), jnp.float32)
    else:
        for block in range(NY):
            top[block] = best_in[block]
    spare = jnp.zeros((BLOCK, PAIR), jnp.float32)
    top[NY], mixed[NY], best[NY] = spare, spare, spare
    for copy in copies:
        copy.wait()

    def score(j, block, row):
        s = lax.dot_general(q_ref[block], kv[row], (((1,), (1,)), ((), ())), preferred_element_type=jnp.float32)
        scores[j] = s
        top[block] = jnp.maximum(top[block], jnp.maximum(s[:, :PAIR], s[:, PAIR:]))

    each_pair(score)

    for block in range(NY):
        new = jnp.broadcast_to(jnp.max(top[block], axis=1, keepdims=True), (BLOCK, PAIR))
        if best_in is not None:
            mixed[block] = mixed_in[block] * jnp.exp2((best_in[block] - new) * EXP2_SCALE)
        best[block] = new

    low = low_lanes((BLOCK, PAIR))

    def mix(j, block, row):
        peak = best[block]
        s = scores[j]
        weights = jnp.concatenate([s[:, :PAIR] - peak, s[:, PAIR:] - peak], axis=1)
        weights = jnp.exp2(weights * EXP2_SCALE).astype(jnp.bfloat16)
        values = jnp.where(low, jnp.ones((), jnp.bfloat16), kv[row])
        mixed[block] += jnp.dot(weights, values, preferred_element_type=jnp.float32)

    each_pair(mix)


def fetch(kv_refs, kv, sems):
    copies = [
        pltpu.make_async_copy(ref, kv.at[pl.ds(i * NY, NY)], sems.at[i]) for i, ref in enumerate(kv_refs)
    ]
    for copy in copies:
        copy.start()
    return copies


def plan_kernel(order_ref, kept_ref, place_ref, mine_ref, q_ref, pairs_ref, counts_ref, where_is):
    list_pairs(order_ref, kept_ref, place_ref, where_is, pairs_ref, counts_ref)
    spread_queries(mine_ref, q_ref)
    q_ref[NY] = jnp.zeros((BLOCK, PAIR), jnp.bfloat16)


def first_kernel(pairs_ref, counts_ref, q_ref, *refs):
    kv_refs = refs[:3]
    best, mixed, kv, scores, top, sems = refs[3:]
    copies = fetch(kv_refs, kv, sems)
    add_pairs(0, copies, pairs_ref, counts_ref, q_ref, kv, None, best, None, mixed, scores, top)


def second_kernel(pairs_ref, counts_ref, q_ref, best_in, mixed_in, *refs):
    kv_refs = refs[:3]
    best, mixed, kv, scores, top, sems = refs[3:]
    copies = fetch(kv_refs, kv, sems)
    add_pairs(1, copies, pairs_ref, counts_ref, q_ref, kv, best_in, best, mixed_in, mixed, scores, top)


def last_kernel(pairs_ref, counts_ref, q_ref, best_in, mixed_in, *refs):
    kv_refs = refs[:2]
    out_ref, best, mixed, kv, scores, top, sems = refs[2:]
    copies = fetch(kv_refs, kv, sems)
    add_pairs(2, copies, pairs_ref, counts_ref, q_ref, kv, best_in, best, mixed_in, mixed, scores, top)
    half = SLICE // 2
    low = low_lanes((NY, half, PAIR))
    for block in range(NY):
        here = mixed[block]
        there = jnp.concatenate([here[:, HD:], here[:, :HD]], axis=1).reshape(NY, SLICE, PAIR)
        here = here.reshape(NY, SLICE, PAIR)
        values = jnp.where(low, there[:, :half], here[:, half:])
        totals = jnp.where(low, here[:, :half], there[:, half:])
        out_ref[pl.ds(block * NY, NY)] = (values / totals).astype(jnp.bfloat16)


VMEM = pl.BlockSpec(memory_space=pltpu.VMEM)
SMEM = pl.BlockSpec(memory_space=pltpu.SMEM)
ANY = pl.BlockSpec(memory_space=pl.ANY)


def pack(q, k, v):
    rows = pltpu.VMEM((SLICE, HEADS * HD), jnp.bfloat16)
    return pl.pallas_call(
        pack_kernel,
        out_shape=pltpu.VMEM((COLS, SLICE + SLICE // 2, PAIR), jnp.bfloat16),
        in_specs=[ANY] * 3,
        out_specs=VMEM,
        scratch_shapes=[rows, rows, rows, pltpu.SemaphoreType.DMA((PARTS, 3))],
        name="pack",
    )(q, k, v)


def unpack(mixed):
    return pl.pallas_call(
        unpack_kernel,
        out_shape=jax.ShapeDtypeStruct((SLICE, HEADS * HD), jnp.bfloat16),
        in_specs=[VMEM],
        out_specs=ANY,
        scratch_shapes=[
            pltpu.VMEM((SLICE, HEADS * HD), jnp.bfloat16),
            pltpu.SemaphoreType.DMA((PARTS,)),
        ],
        name="unpack",
    )(mixed)


STATE = jax.ShapeDtypeStruct((NY + 1, BLOCK, PAIR), jnp.float32)


def stage_scratch(chunks):
    return [
        pltpu.VMEM((chunks * NY, BLOCK, PAIR), jnp.bfloat16),
        pltpu.VMEM((NY * KMAX + UNROLL, BLOCK, BLOCK), jnp.float32),
        pltpu.VMEM((NY + 1, BLOCK, PAIR), jnp.float32),
    ]


def stage_options(share):
    return dict(
        compiler_params=pltpu.CompilerParams(vmem_limit_bytes=36 * 1024 * 1024),
        cost_estimate=pl.CostEstimate(flops=share, bytes_accessed=share, transcendentals=share),
    )


def plan(order, kept, place, mine):
    return pl.pallas_call(
        plan_kernel,
        out_shape=(
            jax.ShapeDtypeStruct((NY + 1, BLOCK, PAIR), jnp.bfloat16),
            pltpu.SMEM((3 * LIST,), jnp.int32),
            pltpu.SMEM((3,), jnp.int32),
        ),
        in_specs=[SMEM] * 3 + [VMEM],
        out_specs=(VMEM, SMEM, SMEM),
        scratch_shapes=[pltpu.SMEM((NB,), jnp.int32)],
        name="plan_pairs",
        **stage_options(1),
    )(order, kept, place, mine)


def attend_first(pairs, counts, q, early):
    return pl.pallas_call(
        first_kernel,
        out_shape=(STATE, STATE),
        in_specs=[SMEM] * 2 + [VMEM] + [ANY] * 3,
        out_specs=(VMEM, VMEM),
        scratch_shapes=stage_scratch(3) + [pltpu.SemaphoreType.DMA((3,))],
        name="attend_early",
        **stage_options(1),
    )(pairs, counts, q, *early)


def attend_second(pairs, counts, q, best, mixed, near):
    return pl.pallas_call(
        second_kernel,
        out_shape=(STATE, STATE),
        in_specs=[SMEM] * 2 + [VMEM] * 3 + [ANY] * 3,
        out_specs=(VMEM, VMEM),
        scratch_shapes=stage_scratch(3) + [pltpu.SemaphoreType.DMA((3,))],
        input_output_aliases={3: 0, 4: 1},
        name="attend_near",
        **stage_options(2),
    )(pairs, counts, q, best, mixed, *near)


def attend_last(pairs, counts, q, best, mixed, far):
    return pl.pallas_call(
        last_kernel,
        out_shape=jax.ShapeDtypeStruct((COLS, SLICE // 2, PAIR), jnp.bfloat16),
        in_specs=[SMEM] * 2 + [VMEM] * 3 + [ANY] * 2,
        out_specs=VMEM,
        scratch_shapes=[pltpu.VMEM((NY + 1, BLOCK, PAIR), jnp.float32)] * 2
        + stage_scratch(2)
        + [pltpu.SemaphoreType.DMA((2,))],
        name="attend_far",
        **stage_options(1),
    )(pairs, counts, q, best, mixed, *far)


def local(queries, key_vectors, value_vectors, frame_order, kept_blocks):
    tm, head = lax.axis_index("tm"), lax.axis_index("head")
    x_here = ((tm >> 1) & 1) * 2 + (head >> 3)
    column = (tm >> 2) * 8 + (head & 7)
    place = jnp.stack([x_here, tm & 1, (column < HEADS).astype(jnp.int32)]).astype(jnp.int32)
    packed = pack(queries, key_vectors, value_vectors)
    mine = lax.all_to_all(packed, AXES, 0, 0, tiled=True, axis_index_groups=COLUMN_GROUPS)
    kv = mine[:, :SLICE].reshape(NY, BLOCK, PAIR)
    swap = lambda t: lax.ppermute(t, AXES, SWAP_CORES)
    onward = lambda t: lax.ppermute(t, AXES, ONWARD)
    near_own = onward(kv)
    twin = swap(kv)
    q, pairs, counts = plan(frame_order, kept_blocks.T, place, mine)
    near_twin = lax.ppermute(kv, AXES, ACROSS)
    near_own, q = lax.optimization_barrier((near_own, q))
    far = onward(near_own)
    best, mixed = attend_first(pairs, counts, q, [kv, twin, near_own])
    near_own, best, mixed = lax.optimization_barrier((near_own, best, mixed))
    near = [near_twin, swap(near_own), swap(near_twin)]
    best, mixed = attend_second(pairs, counts, q, best, mixed, near)
    mixed = attend_last(pairs, counts, q, best, mixed, [far, swap(far)])
    back = lax.all_to_all(mixed, AXES, 0, 0, tiled=True, axis_index_groups=COLUMN_GROUPS)
    return unpack(pltpu.with_memory_space_constraint(back, pltpu.VMEM))


def solution(mesh):
    tokens = P(AXES, None)
    return jax.shard_map(
        local, mesh=mesh, in_specs=(tokens, tokens, tokens, P(), P()), out_specs=tokens, check_vma=False
    )
```
